512 devices in a mesh: adapter: 64 (over x, y, core), tensor: 8 (over z).
Axes of the slice: x: 4, y: 8, z: 8, core: 2. Of those that a mesh axis runs over, the one named last changes fastest.
Arguments:
- tokens: bfloat16 [32768, 8192], P('adapter', 'tensor'), may hold values from -6 to 6
- token_adapter_index: int32 [32768], P('adapter'), may hold values from 0 to 127, as said below
- adapter_stored_row: int32 [128], replicated, may hold values from 0 to 127, as said below
- value_base_weight: bfloat16 [8192, 1024], P('tensor'), may hold values from -0.09375 to 0.09375
- adapter_down_maps: bfloat16 [128, 64, 8192], P('adapter', None, 'tensor'), may hold values from -0.0625 to 0.0625
- adapter_up_maps: bfloat16 [128, 64, 1024], P('adapter', None, 'tensor'), may hold values from -0.75 to 0.75
Outputs:
- values: bfloat16 [32768, 1024], P('adapter', 'tensor')
The draws below stay inside these ranges and needn't reach their ends.
Inputs may be any that keep to these rules, and one draw needn't show every extreme that they name: adapter_stored_row is a permutation; stored row s belongs to owner s // 2. `token_adapter_index`: among the 512 tokens of each index of adapter (consecutive rows), at most 10 have adapters whose stored rows belong to one owner.
All inputs are finite; a program needn't handle non-finite values.
Results may differ from the reference program's by a relative error of at most 0.0053.
Values may be sent and summed in bfloat16 or wider, within the bound.
A program may use at most 64 MiB of HBM per device.

```python
import jax
import jax.numpy as jnp
from jax import lax

MODEL_WIDTH = 8192
VALUE_OUTPUTS = 1024
ADAPTER_RANK = 64
ADAPTERS_HELD = 2
ROWS = 512
GROUPS = 64
ADAPTER_TOTAL = 128
CAP = 10
TOKENS = 32768


def shared_slots(key):
    return jax.random.permutation(key, ADAPTER_TOTAL).astype(jnp.int32)


def draw_adapter_stored_row(key, part):
    slots = shared_slots(key)
    return slots


def draw_token_adapter_index(key, part):
    slots = shared_slots(key)
    key = jax.random.fold_in(key, 23)
    stored = jnp.zeros((ADAPTER_TOTAL,), jnp.int32).at[slots].set(jnp.arange(ADAPTER_TOTAL, dtype=jnp.int32))
    busiest = jax.random.randint(jax.random.fold_in(key, 1), (), 0, GROUPS).astype(jnp.int32)

    def one_device(index):
        device_key = jax.random.fold_in(key, index + 2)
        first_key, second_key, third_key = jax.random.split(device_key, 3)
        others = jax.random.permutation(first_key, (GROUPS - 1) * CAP)[:ROWS - CAP].astype(jnp.int32)
        other_owner = (busiest + 1 + others // CAP) % GROUPS
        owners = jnp.concatenate([jnp.full((CAP,), 1, jnp.int32) * busiest, other_owner])
        owners = jax.random.permutation(second_key, owners)
        within = jax.random.randint(third_key, (ROWS,), 0, ADAPTERS_HELD).astype(jnp.int32)
        return stored[owners * ADAPTERS_HELD + within]
    return jax.vmap(one_device)(jnp.arange(GROUPS, dtype=jnp.int32)).reshape(-1)


def spiked(drawn, stream_key, source, target, shards_of, factor):
    owner, partner = [(jnp.arange(drawn.shape[axis_at]) // (drawn.shape[axis_at] // shards_of)).reshape([-1 if axis == axis_at else 1 for axis in range(drawn.ndim)]) for axis_at in (source, target)]
    chosen = jax.random.permutation(stream_key, shards_of)[partner]
    strong = (owner == chosen) | (owner == (partner + shards_of // 2) % shards_of)
    return jnp.where(strong, factor * drawn, drawn)


def block_levels(own_key, extent, cuts, low, top_value):
    level = 1.0
    for axis_at, parts in cuts:
        draws = jax.random.uniform(jax.random.fold_in(jax.random.fold_in(own_key, 6), axis_at), (parts,), jnp.float32, low / len(cuts), top_value / len(cuts))
        level = level * jnp.repeat(jnp.exp(draws), extent[axis_at] // parts).reshape((-1,) + (1,) * (len(extent) - 1 - axis_at))
    return level


def normal_values(own_key, shape, width, bound, pieces=(), kind=jnp.bfloat16):
    gain = block_levels(own_key, shape, pieces, -0.22, 0.18) if pieces else 1.0
    drawn = jax.random.normal(own_key, shape, jnp.float32) * width * gain
    return jnp.minimum(jnp.maximum(drawn, -bound), bound).astype(kind)


def bell_draw_with(stream_key, dims, width, bound, cuts, heavy, kind=jnp.bfloat16):
    values = width * jax.random.normal(stream_key, dims, jnp.float32)
    if cuts:
        values = values * block_levels(stream_key, dims, cuts, -0.22, 0.18)
    return jnp.clip(spiked(values, jax.random.fold_in(stream_key, 3), *heavy), -bound, bound).astype(kind)


def setup_inputs(seed: int = 0) -> dict:
    streams_of = jax.random.split(jax.random.key(seed), 7)
    tokens = normal_values(streams_of[0], (TOKENS, MODEL_WIDTH), 1.0, 6.0, ((0, 64), (1, 8)))
    token_adapter_index = draw_token_adapter_index(jax.random.fold_in(streams_of[6], 71), 0)
    adapter_stored_row = draw_adapter_stored_row(jax.random.fold_in(streams_of[6], 71), 0)
    value_base_weight = bell_draw_with(streams_of[3], (MODEL_WIDTH, VALUE_OUTPUTS), MODEL_WIDTH ** -0.5, 0.09375, ((0, 8),), (0, 1, 8, 2.0))
    adapter_down_maps = normal_values(streams_of[4], (ADAPTER_TOTAL, ADAPTER_RANK, MODEL_WIDTH), MODEL_WIDTH ** -0.5, 0.0625, ((0, 64), (2, 8)))
    adapter_up_maps = normal_values(streams_of[5], (ADAPTER_TOTAL, ADAPTER_RANK, VALUE_OUTPUTS), ADAPTER_RANK ** -0.5, 0.75, ((0, 64), (2, 8)))
    return {"tokens": tokens, "token_adapter_index": token_adapter_index, "adapter_stored_row": adapter_stored_row, "value_base_weight": value_base_weight, "adapter_down_maps": adapter_down_maps, "adapter_up_maps": adapter_up_maps}


adapter_scale = 2.0


def reference(tokens, token_adapter_index, adapter_stored_row, value_base_weight, adapter_down_maps, adapter_up_maps):
    slot = adapter_stored_row[token_adapter_index].astype(jnp.int32)
    owner = slot // ADAPTERS_HELD
    within = slot % ADAPTERS_HELD
    buffer_rows = GROUPS * CAP

    def visit(total, token_group):
        chosen = owner == token_group
        picked = jnp.nonzero(chosen, size=buffer_rows, fill_value=0)[0].astype(jnp.int32)
        live = jnp.arange(buffer_rows) < jnp.sum(chosen.astype(jnp.int32))
        gathered = tokens[picked].astype(jnp.float32)
        down_matrix = lax.dynamic_slice_in_dim(adapter_down_maps, (token_group * ADAPTERS_HELD).astype(jnp.int32), ADAPTERS_HELD, 0).astype(jnp.float32)
        up_matrix = lax.dynamic_slice_in_dim(adapter_up_maps, (token_group * ADAPTERS_HELD).astype(jnp.int32), ADAPTERS_HELD, 0)
        select = ((within[picked][:, None] == jnp.arange(ADAPTERS_HELD)[None, :]) & live[:, None]).astype(jnp.float32)
        partial_all = jnp.einsum("yn,vln->yvl", gathered, down_matrix)
        shrunk = jnp.sum(partial_all * select[:, :, None], axis=1).astype(jnp.bfloat16)
        spread_rows = (select[:, :, None] * shrunk[:, None, :].astype(jnp.float32)).reshape(buffer_rows, ADAPTERS_HELD * ADAPTER_RANK).astype(jnp.bfloat16)
        adapter_update = (adapter_scale * jnp.dot(spread_rows, up_matrix.reshape(ADAPTERS_HELD * ADAPTER_RANK, VALUE_OUTPUTS), preferred_element_type=jnp.float32)).astype(jnp.bfloat16)
        return total.at[picked].add(adapter_update), None

    start = jnp.zeros((TOKENS, VALUE_OUTPUTS), jnp.bfloat16)
    total, unused = lax.scan(visit, start, jnp.arange(GROUPS, dtype=jnp.int32))
    base = jnp.dot(tokens, value_base_weight, preferred_element_type=jnp.float32)
    return (base + total.astype(jnp.float32)).astype(jnp.bfloat16)
```

```python
import jax
import jax.numpy as jnp
from jax import lax
from jax.experimental import pallas as pl
from jax.experimental.pallas import tpu as pltpu
from jax.sharding import PartitionSpec as P

MESH = pl.DeviceIdType.MESH
BF16, F32, I32 = jnp.bfloat16, jnp.float32, jnp.int32

X, Y, CORES, Z = 4, 8, 2, 8
ROWS, WIDTH, OUT = 512, 1024, 128
CAP, RANK = 10, 64
SLOTS = CORES * CAP
BLOCK = Y * SLOTS
ALL = X * BLOCK
SUBS = 4
HELD = 2 * RANK
SUB = HELD // SUBS
HALF = ROWS // 2
PIECE = BLOCK // 4
PADDED = 48
OFFSETS = (0, 1, 7, 2, 6, 3, 5, 4)
adapter_scale = 2.0


def dot(a, b):
    return jnp.dot(a, b, preferred_element_type=F32)


def dot_nt(a, b):
    return lax.dot_general(a, b, (((1,), (1,)), ((), ())), preferred_element_type=F32)


def dot_tn(a, b):
    return lax.dot_general(a, b, (((0,), (0,)), ((), ())), preferred_element_type=F32)


def iota(shape, axis):
    return lax.broadcasted_iota(I32, shape, axis)


def kernel(
    idx_ref,
    stored_ref,
    tok_hbm,
    w_hbm,
    down_hbm,
    up_hbm,
    out_ref,
    tok,
    w,
    down,
    up,
    perm,
    send_rows,
    rows,
    send_place,
    place,
    part,
    ring_out,
    ring_in,
    acc,
    packed,
    sums,
    shrunk,
    back_out,
    back,
    sel,
    delta,
    local_sem,
    y_send,
    y_recv,
    core_send,
    core_recv,
    up_send,
    up_recv,
    x_send,
    x_recv,
    ring_send,
    ring_recv,
    sum_send,
    sum_recv,
    all_send,
    all_recv,
    back_send,
    back_recv,
):
    a = lax.axis_index("adapter")
    z = lax.axis_index("tensor")
    x, y, c = a // (Y * CORES), (a // CORES) % Y, a % CORES

    def device(dx=0, dy=0, dc=0, dz=0):
        ax = lax.rem(x + (dx + X), X)
        ay = lax.rem(y + (dy + Y), Y)
        ac = lax.rem(c + dc, CORES)
        return ((ax * Y + ay) * CORES + ac, lax.rem(z + (dz + Z), Z))

    def remote(src, dst, send, recv, **to):
        return pltpu.make_async_remote_copy(
            src_ref=src,
            dst_ref=dst,
            send_sem=send,
            recv_sem=recv,
            device_id=device(**to),
            device_id_type=MESH,
        )

    started = []

    def go(copy):
        copy.start()
        started.append(copy)

    barrier = pltpu.get_barrier_semaphore()
    partners = [dict(dc=1)]
    partners += [dict(dx=d) for d in range(1, X)]
    partners += [dict(dy=d) for d in range(1, Y)]
    partners += [dict(dz=d) for d in range(1, Z)]
    for to in partners:
        pl.semaphore_signal(barrier, inc=1, device_id=device(**to), device_id_type=MESH)
    load_down = pltpu.make_async_copy(down_hbm, down.at[0, c], local_sem.at[0])
    load_tok = pltpu.make_async_copy(tok_hbm, tok, local_sem.at[1])
    load_w = pltpu.make_async_copy(w_hbm, w, local_sem.at[2])
    load_up = pltpu.make_async_copy(up_hbm, up.at[c, 0], local_sem.at[3])
    for load in (load_down, load_tok, load_w, load_up):
        load.start()

    def y_slot(way, hop):
        return (Y - hop) % Y if way == 0 else hop

    def y_copy(way, hop, sub):
        span = pl.ds(sub * SUB, SUB)
        return remote(
            down.at[y_slot(way, hop - 1), c, span],
            down.at[y_slot(way, hop), c, span],
            y_send.at[way, hop - 1, sub],
            y_recv.at[way, hop - 1, sub],
            dy=1 if way == 0 else -1,
        )

    def y_subs(way, hop):
        order = (0, 1, 2, 3) if way == 0 else (2, 3, 0, 1)
        return order[:2] if hop == Y // 2 else order

    def core_copy(slot):
        return remote(
            down.at[slot, c], down.at[slot, c], core_send.at[slot], core_recv.at[slot], dc=1
        )

    def core_arrival(slot):
        return remote(
            down.at[slot, 1 - c], down.at[slot, 1 - c], core_send.at[slot], core_recv.at[slot], dc=1
        )

    idx = idx_ref[...]
    stored = jnp.broadcast_to(stored_ref[...].astype(F32), (8, 128)).astype(BF16)
    lookup = jnp.where(iota((128, ROWS), 0) == idx, 1.0, 0.0).astype(BF16)
    slot = dot(stored, lookup)[0:1].astype(I32)
    owner = slot // 2
    within = slot - owner * 2
    member = jnp.where(iota((64, ROWS), 0) == owner, 1.0, 0.0)
    earlier = jnp.where(iota((ROWS, ROWS), 0) < iota((ROWS, ROWS), 1), 1.0, 0.0).astype(BF16)
    before = jnp.sum(dot(member.astype(BF16), earlier) * member, axis=0, keepdims=True)
    owner_x, owner_y, owner_c = owner // 16, (owner // 2) & 7, owner & 1
    step_x = (owner_x - x) & 3
    step_y = (owner_y - y) & 7
    position = jnp.where(
        step_y == 0, 0, jnp.where(step_y <= 4, 2 * step_y - 1, 2 * (8 - step_y))
    )
    target = step_x * BLOCK + position * SLOTS + owner_c * CAP + before.astype(I32)
    perm[...] = jnp.where(iota((ALL + 128, ROWS), 0) == target, 1.0, 0.0).astype(BF16)
    within16 = jnp.broadcast_to(within.astype(F32), (16, ROWS)).astype(BF16)

    load_down.wait()
    load_up.wait()
    pl.semaphore_wait(barrier, len(partners))
    for i in range(SUBS):
        for way in range(2):
            go(y_copy(way, 1, y_subs(way, 1)[i]))
    go(core_copy(0))

    def x_copies(dx):
        return (
            remote(
                send_rows.at[dx - 1], rows.at[dx], x_send.at[0, dx - 1], x_recv.at[0, dx - 1], dx=dx
            ),
            remote(
                send_place.at[dx - 1],
                place.at[dx],
                x_send.at[1, dx - 1],
                x_recv.at[1, dx - 1],
                dx=dx,
            ),
        )

    load_tok.wait()
    for dx in (2, 1, 3, 0):
        block = dot(perm[dx * BLOCK : (dx + 1) * BLOCK, :], tok[...]).astype(BF16)
        where = dot_nt(within16, perm[dx * BLOCK : dx * BLOCK + 256, :]).astype(BF16)
        if dx:
            send_rows[dx - 1] = block
            send_place[dx - 1] = where
            for copy in x_copies(dx):
                go(copy)
        else:
            rows[0] = block
            place[0] = where

    def product(m):
        k = lax.rem(z + m, Z)
        part[m] = dot(tok[...], w[:, pl.ds(pl.multiple_of(k * OUT, OUT), OUT)])

    def ring_copy(way, step, half):
        return remote(
            ring_out.at[way, step - 1, half],
            ring_in.at[way, step - 1, half],
            ring_send.at[way, step - 1, half],
            ring_recv.at[way, step - 1, half],
            dz=1 if way == 0 else -1,
        )

    def ring_m(way, step):
        return 5 - step if way == 0 else 3 + step

    def ring_pass(way, step, half, arrived):
        m = ring_m(way, step)
        value = part[m, half * HALF : (half + 1) * HALF, :]
        if arrived:
            ring_copy(way, step - 1, half).wait_recv()
            value = value + ring_in[way, step - 2, half].astype(F32)
        ring_out[way, step - 1, half] = value.astype(BF16)
        go(ring_copy(way, step, half))

    load_w.wait()
    product(4)
    for way in range(2):
        ring_pass(way, 1, way, False)
    product(3)
    ring_pass(0, 2, 1, False)
    product(5)
    ring_pass(1, 2, 0, False)

    def y_forward(hop, i):
        for way in range(2):
            sub = y_subs(way, hop)[i]
            y_copy(way, hop, sub).wait_recv()
            if hop < Y // 2 and sub in y_subs(way, hop + 1):
                go(y_copy(way, hop + 1, sub))

    def ring_step(step):
        for way in range(2):
            first = way
            halves = (first,) if step == 1 else (first, 1 - first)
            for half in halves:
                ring_pass(way, step + 1, half, True)

    fillers = {(1, 0): (2, 6), (1, 1): (1, 7), (1, 2): (0,)}
    for hop in range(1, 4):
        for i in range(SUBS):
            y_forward(hop, i)
            for m in fillers.get((hop, i), ()):
                product(m)
            if i == 2:
                ring_step(hop)
        go(core_copy(y_slot(0, hop)))
        go(core_copy(y_slot(1, hop)))

    def up_copy(dy):
        return remote(
            up.at[c, 0], up.at[c, Y - dy], up_send.at[dy - 1], up_recv.at[dy - 1], dy=dy
        )

    for dy in (4, 3, 5, 2, 6, 1, 7):
        go(up_copy(dy))

    acc[...] = jnp.zeros(acc.shape, F32)
    eye = iota((BLOCK, 256), 0) == iota((BLOCK, 256), 1)
    ones = jnp.ones((256, 128), BF16)
    for dx in (0, 1, 3, 2):
        if dx:
            for copy in x_copies(dx):
                copy.wait_recv()
        spread = jnp.where(eye, place[dx, 0:1, :].astype(F32), 0.0).astype(BF16)
        sel[dx] = jnp.where(
            dot(spread, ones).astype(I32) == iota((BLOCK, 128), 1) // RANK, 1.0, 0.0
        )

    def window(p):
        return (p * SLOTS) // 16 * 16

    def core_masks(p):
        row = window(p) + iota((X, 32, 128), 1) - p * SLOTS
        return [
            jnp.where((row >= k * CAP) & (row < (k + 1) * CAP), 1.0, 0.0) for k in range(CORES)
        ]

    def down_project(p):
        slot = OFFSETS[p]
        core_arrival(slot).wait_recv()
        lo = window(p)
        mine = rows[:, lo : lo + 32, :].reshape(X * 32, WIDTH)
        got = dot_nt(mine, down[slot].reshape(CORES * HELD, WIDTH)).reshape(X, 32, 256)
        first, second = core_masks(p)
        kept = got[:, :, :128] * first + got[:, :, 128:] * second
        acc[:, lo : lo + 32, :] += kept * sel[:, lo : lo + 32, :]

    for p in range(7):
        down_project(p)
    for i in range(2):
        y_forward(4, i)
    go(core_copy(4))
    for way in range(2):
        for half in range(2):
            ring_copy(way, 4, half).wait_recv()
            span = slice(half * HALF, (half + 1) * HALF)
            part[0, span, :] += ring_in[way, 3, half].astype(F32)
    down_project(7)

    both = acc[...]
    both = both + jnp.concatenate([both[:, :, RANK:], both[:, :, :RANK]], axis=2)
    low = iota((BLOCK, 128), 1) < RANK
    for pair in range(2):
        side = jnp.where(low, both[2 * pair], both[2 * pair + 1])
        packed[4 * pair : 4 * pair + 4] = side.reshape(4, PIECE, 128)

    def sum_copy(dz):
        return remote(
            packed.at[lax.rem(z + dz, Z)],
            sums.at[dz - 1],
            sum_send.at[dz - 1],
            sum_recv.at[dz - 1],
            dz=dz,
        )

    far_first = (4, 3, 5, 2, 6, 1, 7)
    for dz in far_first:
        go(sum_copy(dz))
    for dy in (1, 7, 2, 6, 3, 5, 4):
        up_copy(dy).wait_recv()
    up_swap = remote(up.at[c], up.at[c], up_send.at[7], up_recv.at[7], dc=1)
    go(up_swap)
    total = packed[z]
    for dz in (1, 7, 2, 6, 3, 5, 4):
        sum_copy(dz).wait_recv()
        total = total + sums[dz - 1]
    shrunk[z] = jnp.concatenate([total, jnp.zeros((PADDED - PIECE, 128), F32)], axis=0).astype(BF16)

    def all_copy(dz):
        return remote(
            shrunk.at[z], shrunk.at[z], all_send.at[dz - 1], all_recv.at[dz - 1], dz=dz
        )

    def all_arrival(dz):
        k = lax.rem(z + (Z - dz), Z)
        return remote(
            shrunk.at[k], shrunk.at[k], all_send.at[dz - 1], all_recv.at[dz - 1], dz=dz
        )

    for dz in far_first:
        go(all_copy(dz))
    remote(up.at[1 - c], up.at[1 - c], up_send.at[7], up_recv.at[7], dc=1).wait_recv()
    for dz in (1, 7, 2, 6, 3, 5, 4):
        all_arrival(dz).wait_recv()

    for pair in range(2):
        whole = shrunk[4 * pair : 4 * pair + 4].astype(F32)[:, :PIECE, :].reshape(BLOCK, 128)
        swapped = jnp.concatenate([whole[:, RANK:], whole[:, :RANK]], axis=1)
        acc[2 * pair] = jnp.where(low, whole, swapped) * sel[2 * pair]
        acc[2 * pair + 1] = jnp.where(low, swapped, whole) * sel[2 * pair + 1]
    delta[...] = jnp.zeros(delta.shape, F32)
    for p in range(8):
        lo = window(p)
        mine = acc[:, lo : lo + 32, :]
        first, second = core_masks(p)
        wide = jnp.concatenate([mine * first, mine * second], axis=2).astype(BF16)
        maps = up[:, OFFSETS[p]].reshape(CORES * HELD, OUT)
        got = dot(wide.reshape(X * 32, 256), maps).reshape(X, 32, OUT)
        delta[:, lo : lo + 32, :] += got

    def back_copy(dx):
        return remote(
            back_out.at[dx - 1], back.at[dx], back_send.at[dx - 1], back_recv.at[dx - 1], dx=-dx
        )

    for dx in (2, 1, 3, 0):
        block = delta[dx]
        block = (adapter_scale * block).astype(BF16)
        if dx:
            back_out[dx - 1] = block
            go(back_copy(dx))
        else:
            back[0] = block
    for dx in (1, 3, 2):
        back_copy(dx).wait_recv()
    mine = dot_tn(perm[0:ALL, :], back[...].reshape(ALL, OUT))
    out_ref[...] = (part[0] + mine).astype(BF16)

    for copy in started:
        copy.wait_send()


def local(
    tokens,
    token_adapter_index,
    adapter_stored_row,
    value_base_weight,
    adapter_down_maps,
    adapter_up_maps,
):
    vmem = pl.BlockSpec(memory_space=pltpu.VMEM)
    hbm = pl.BlockSpec(memory_space=pl.ANY)
    dma = pltpu.SemaphoreType.DMA
    return pl.pallas_call(
        kernel,
        out_shape=jax.ShapeDtypeStruct((ROWS, OUT), BF16),
        in_specs=[vmem, vmem, hbm, hbm, hbm, hbm],
        out_specs=vmem,
        scratch_shapes=[
            pltpu.VMEM((ROWS, WIDTH), BF16),
            pltpu.VMEM((WIDTH, Z * OUT), BF16),
            pltpu.VMEM((Y, CORES, HELD, WIDTH), BF16),
            pltpu.VMEM((CORES, Y, HELD, OUT), BF16),
            pltpu.VMEM((ALL + 128, ROWS), BF16),
            pltpu.VMEM((X - 1, BLOCK, WIDTH), BF16),
            pltpu.VMEM((X, BLOCK, WIDTH), BF16),
            pltpu.VMEM((X - 1, 16, 256), BF16),
            pltpu.VMEM((X, 16, 256), BF16),
            pltpu.VMEM((Z, ROWS, OUT), F32),
            pltpu.VMEM((2, 4, 2, HALF, OUT), BF16),
            pltpu.VMEM((2, 4, 2, HALF, OUT), BF16),
            pltpu.VMEM((X, BLOCK, 128), F32),
            pltpu.VMEM((Z, PIECE, 128), F32),
            pltpu.VMEM((Z - 1, PIECE, 128), F32),
            pltpu.VMEM((Z, PADDED, 128), BF16),
            pltpu.VMEM((X - 1, BLOCK, OUT), BF16),
            pltpu.VMEM((X, BLOCK, OUT), BF16),
            pltpu.VMEM((X, BLOCK, 128), F32),
            pltpu.VMEM((X, BLOCK, OUT), F32),
            dma((4,)),
            dma((2, 4, SUBS)),
            dma((2, 4, SUBS)),
            dma((Y,)),
            dma((Y,)),
            dma((Y,)),
            dma((Y,)),
            dma((2, X - 1)),
            dma((2, X - 1)),
            dma((2, 4, 2)),
            dma((2, 4, 2)),
            dma((Z - 1,)),
            dma((Z - 1,)),
            dma((Z - 1,)),
            dma((Z - 1,)),
            dma((X - 1,)),
            dma((X - 1,)),
        ],
        compiler_params=pltpu.CompilerParams(
            collective_id=0, has_side_effects=True, vmem_limit_bytes=60 << 20
        ),
        cost_estimate=pl.CostEstimate(
            flops=5_000_000_000, bytes_accessed=3_700_000, transcendentals=0
        ),
    )(
        token_adapter_index.reshape(1, ROWS),
        adapter_stored_row.reshape(1, -1),
        tokens,
        value_base_weight,
        adapter_down_maps.reshape(HELD, WIDTH),
        adapter_up_maps.reshape(HELD, OUT),
    )


def solution(mesh):
    return jax.shard_map(
        local,
        mesh=mesh,
        in_specs=(
            P("adapter", "tensor"),
            P("adapter"),
            P(),
            P("tensor", None),
            P("adapter", None, "tensor"),
            P("adapter", None, "tensor"),
        ),
        out_specs=P("adapter", "tensor"),
        check_vma=False,
    )
```

```python
import jax
import jax.numpy as jnp
from jax import lax
from jax.experimental import pallas as pl
from jax.experimental.pallas import tpu as pltpu
from jax.sharding import PartitionSpec as P

MESH = pl.DeviceIdType.MESH
BF16, F32, I32 = jnp.bfloat16, jnp.float32, jnp.int32

X, Y, CORES, Z = 4, 8, 2, 8
ROWS, WIDTH, OUT = 512, 1024, 128
CAP, RANK = 10, 64
FAR = Y // 2
LATE = 24
SLOTS = CORES * CAP
BLOCK = Y * SLOTS
ALL = X * BLOCK
SUBS = 4
HELD = 2 * RANK
SUB = HELD // SUBS
HALF = ROWS // 2
PIECE = BLOCK // 4
PADDED = 48
OFFSETS = (0, 1, 7, 2, 6, 3, 5, 4)
adapter_scale = 2.0


def dot(a, b):
    return jnp.dot(a, b, preferred_element_type=F32)


def dot_nt(a, b):
    return lax.dot_general(a, b, (((1,), (1,)), ((), ())), preferred_element_type=F32)


def iota(shape, axis):
    return lax.broadcasted_iota(I32, shape, axis)


def kernel(
    idx_hbm,
    stored_hbm,
    tok_hbm,
    w_hbm,
    down_hbm,
    up_hbm,
    out_ref,
    idx_ref,
    stored_ref,
    tok,
    w,
    down,
    up,
    perm,
    perm_t,
    send_rows,
    rows,
    send_place,
    place,
    part,
    ring_out,
    ring_in,
    acc,
    packed,
    sums,
    shrunk,
    late_out,
    late_in,
    back_out,
    back,
    sel,
    delta,
    local_sem,
    y_send,
    y_recv,
    core_send,
    core_recv,
    up_send,
    up_recv,
    x_send,
    x_recv,
    ring_send,
    ring_recv,
    sum_send,
    sum_recv,
    all_send,
    all_recv,
    late_send,
    late_recv,
    back_send,
    back_recv,
):
    a = lax.axis_index("adapter")
    z = lax.axis_index("tensor")
    x, y, c = a // (Y * CORES), (a // CORES) % Y, a % CORES

    def device(dx=0, dy=0, dc=0, dz=0):
        ax = lax.rem(x + (dx + X), X)
        ay = lax.rem(y + (dy + Y), Y)
        ac = lax.rem(c + dc, CORES)
        return ((ax * Y + ay) * CORES + ac, lax.rem(z + (dz + Z), Z))

    def remote(src, dst, send, recv, **to):
        return pltpu.make_async_remote_copy(
            src_ref=src,
            dst_ref=dst,
            send_sem=send,
            recv_sem=recv,
            device_id=device(**to),
            device_id_type=MESH,
        )

    started, slow = [], []

    def go(copy):
        copy.start()
        started.append(copy)

    barrier = pltpu.get_barrier_semaphore()
    partners = [dict(dc=1)]
    partners += [dict(dx=d) for d in range(1, X)]
    partners += [dict(dy=d) for d in range(1, Y)]
    partners += [dict(dz=d) for d in range(1, Z)]
    for to in partners:
        pl.semaphore_signal(barrier, inc=1, device_id=device(**to), device_id_type=MESH)
    load_idx = pltpu.make_async_copy(idx_hbm, idx_ref, local_sem.at[4])
    load_stored = pltpu.make_async_copy(stored_hbm, stored_ref, local_sem.at[5])
    load_down = pltpu.make_async_copy(down_hbm, down.at[0, c], local_sem.at[0])
    load_tok = pltpu.make_async_copy(tok_hbm, tok, local_sem.at[1])
    load_w = pltpu.make_async_copy(w_hbm, w, local_sem.at[2])
    load_up = pltpu.make_async_copy(up_hbm, up.at[c, 0], local_sem.at[3])
    for load in (load_down, load_idx, load_stored, load_tok, load_up, load_w):
        load.start()

    def y_slot(way, hop):
        return (Y - hop) % Y if way == 0 else hop

    def y_copy(way, hop, sub):
        span = pl.ds(sub * SUB, SUB)
        return remote(
            down.at[y_slot(way, hop - 1), c, span],
            down.at[y_slot(way, hop), c, span],
            y_send.at[way, hop - 1, sub],
            y_recv.at[way, hop - 1, sub],
            dy=1 if way == 0 else -1,
        )

    def y_subs(way, hop):
        first, last = range(SUBS // 2), range(SUBS // 2, SUBS)
        order = (*first, *last) if way == 0 else (*last, *first)
        return order[: SUBS // 2] if hop == Y // 2 else order

    def core_copy(slot):
        return remote(
            down.at[slot, c], down.at[slot, c], core_send.at[slot], core_recv.at[slot], dc=1
        )

    def core_arrival(slot):
        return remote(
            down.at[slot, 1 - c], down.at[slot, 1 - c], core_send.at[slot], core_recv.at[slot], dc=1
        )

    load_down.wait()
    pl.semaphore_wait(barrier, len(partners))
    for i in range(SUBS):
        for way in range(2):
            go(y_copy(way, 1, y_subs(way, 1)[i]))

    def piece_copy(sub, core):
        span = pl.ds(sub * SUB, SUB)
        return remote(
            down.at[FAR, core, span],
            down.at[FAR, core, span],
            core_send.at[Y + sub],
            core_recv.at[Y + sub],
            dc=1,
        )

    load_idx.wait()
    load_stored.wait()
    idx = idx_ref[...]
    stored = jnp.broadcast_to(stored_ref[...].astype(F32), (8, 128)).astype(BF16)
    lookup = jnp.where(iota((128, ROWS), 0) == idx, 1.0, 0.0).astype(BF16)
    slot = dot(stored, lookup)[0:1].astype(I32)
    owner = slot // 2
    within = slot - owner * 2
    member = jnp.where(iota((64, ROWS), 0) == owner, 1.0, 0.0)
    earlier = jnp.where(iota((ROWS, ROWS), 0) < iota((ROWS, ROWS), 1), 1.0, 0.0).astype(BF16)
    before = jnp.sum(dot(member.astype(BF16), earlier) * member, axis=0, keepdims=True)
    owner_x, owner_y, owner_c = owner // 16, (owner // 2) & 7, owner & 1
    step_x = (owner_x - x) & 3
    step_y = (owner_y - y) & 7
    position = jnp.where(
        step_y == 0, 0, jnp.where(step_y <= 4, 2 * step_y - 1, 2 * (8 - step_y))
    )
    target = step_x * BLOCK + position * SLOTS + owner_c * CAP + before.astype(I32)
    perm[...] = jnp.where(iota((ALL + 128, ROWS), 0) == target, 1.0, 0.0).astype(BF16)
    within16 = jnp.broadcast_to(within.astype(F32), (16, ROWS)).astype(BF16)

    def x_copies(dx):
        return (
            remote(
                send_rows.at[dx - 1], rows.at[dx], x_send.at[0, dx - 1], x_recv.at[0, dx - 1], dx=dx
            ),
            remote(
                send_place.at[dx - 1],
                place.at[dx],
                x_send.at[1, dx - 1],
                x_recv.at[1, dx - 1],
                dx=dx,
            ),
        )

    load_tok.wait()
    for dx in (1, 3, 2, 0):
        block = dot(perm[dx * BLOCK : (dx + 1) * BLOCK, :], tok[...]).astype(BF16)
        where = dot_nt(within16, perm[dx * BLOCK : dx * BLOCK + 256, :]).astype(BF16)
        if dx:
            send_rows[dx - 1] = block
            send_place[dx - 1] = where
            for copy in x_copies(dx):
                copy.start()
                slow.append(copy)
        else:
            rows[0] = block
            place[0] = where

    def product(m):
        k = lax.rem(z + m, Z)
        part[m] = dot(tok[...], w[:, pl.ds(pl.multiple_of(k * OUT, OUT), OUT)])

    def ring_copy(way, step, half):
        return remote(
            ring_out.at[way, step - 1, half],
            ring_in.at[way, step - 1, half],
            ring_send.at[way, step - 1, half],
            ring_recv.at[way, step - 1, half],
            dz=1 if way == 0 else -1,
        )

    def ring_m(way, step):
        return 5 - step if way == 0 else 3 + step

    def ring_pass(way, step, half, arrived):
        m = ring_m(way, step)
        value = part[m, half * HALF : (half + 1) * HALF, :]
        if arrived:
            ring_copy(way, step - 1, half).wait_recv()
            value = value + ring_in[way, step - 2, half].astype(F32)
        ring_out[way, step - 1, half] = value.astype(BF16)
        go(ring_copy(way, step, half))

    go(core_copy(0))
    load_up.wait()
    load_w.wait()
    product(4)
    for way in range(2):
        ring_pass(way, 1, way, False)
    product(3)
    ring_pass(0, 2, 1, False)
    product(5)
    ring_pass(1, 2, 0, False)

    def y_forward(hop, i):
        for way in range(2):
            sub = y_subs(way, hop)[i]
            y_copy(way, hop, sub).wait_recv()
            if hop == FAR:
                go(piece_copy(sub, c))
            elif sub in y_subs(way, hop + 1):
                go(y_copy(way, hop + 1, sub))

    def ring_step(step):
        for way in range(2):
            first = way
            halves = (first,) if step == 1 else (first, 1 - first)
            for half in halves:
                ring_pass(way, step + 1, half, True)

    def settle():
        while started:
            started.pop(0).wait_send()

    fillers = {(1, 0): (2, 6), (1, 1): (1, 7, 0)}
    for hop in range(1, 4):
        for i in range(SUBS):
            y_forward(hop, i)
            for m in fillers.get((hop, i), ()):
                product(m)
            if i == SUBS // 2:
                ring_step(hop)
        recent = started[-10:]
        del started[-10:]
        settle()
        started.extend(recent)
        go(core_copy(y_slot(0, hop)))
        go(core_copy(y_slot(1, hop)))
        if hop == 1:
            perm_t[...] = jnp.transpose(perm[0:ALL, :])

    def up_copy(dy):
        return remote(
            up.at[c, 0], up.at[c, Y - dy], up_send.at[dy - 1], up_recv.at[dy - 1], dy=dy
        )


    acc[...] = jnp.zeros(acc.shape, F32)
    eye = iota((BLOCK, 256), 0) == iota((BLOCK, 256), 1)
    ones = jnp.ones((256, 128), BF16)
    for dx in (0, 1, 3, 2):
        if dx:
            for copy in x_copies(dx):
                copy.wait_recv()
        spread = jnp.where(eye, place[dx, 0:1, :].astype(F32), 0.0).astype(BF16)
        sel[dx] = jnp.where(
            dot(spread, ones).astype(I32) == iota((BLOCK, 128), 1) // RANK, 1.0, 0.0
        )

    def window(p):
        return (p * SLOTS) // 16 * 16

    def core_masks(p):
        row = window(p) + iota((X, 32, 128), 1) - p * SLOTS
        return [
            jnp.where((row >= k * CAP) & (row < (k + 1) * CAP), 1.0, 0.0) for k in range(CORES)
        ]

    def down_project(p):
        slot = OFFSETS[p]
        if slot == FAR:
            for sub in range(SUBS):
                piece_copy(sub, 1 - c).wait_recv()
        else:
            core_arrival(slot).wait_recv()
        lo = window(p)
        mine = rows[:, lo : lo + 32, :].reshape(X * 32, WIDTH)
        got = dot_nt(mine, down[slot].reshape(CORES * HELD, WIDTH)).reshape(X, 32, 256)
        first, second = core_masks(p)
        kept = got[:, :, :128] * first + got[:, :, 128:] * second
        return kept * sel[:, lo : lo + 32, :]

    for p in range(7):
        lo = window(p)
        acc[:, lo : lo + 32, :] += down_project(p)

    def side_by_side(found):
        whole = found + jnp.concatenate([found[:, :, RANK:], found[:, :, :RANK]], axis=2)
        low = iota(whole.shape[1:], 1) < RANK
        return [jnp.where(low, whole[2 * pair], whole[2 * pair + 1]) for pair in range(2)]

    for pair, side in enumerate(side_by_side(acc[...])):
        packed[4 * pair : 4 * pair + 4] = side.reshape(4, PIECE, 128)

    def sum_copy(dz):
        return remote(
            packed.at[lax.rem(z + dz, Z)],
            sums.at[dz - 1],
            sum_send.at[dz - 1],
            sum_recv.at[dz - 1],
            dz=dz,
        )

    far_first = (4, 3, 5, 2, 6, 1, 7)
    for dz in far_first:
        go(sum_copy(dz))
    def late_copy(dz):
        return remote(
            late_out, late_in.at[dz - 1], late_send.at[dz - 1], late_recv.at[dz - 1], dz=dz
        )

    for i in range(SUBS // 2):
        y_forward(FAR, i)
    for dy in far_first:
        go(up_copy(dy))
    for pair, side in enumerate(side_by_side(down_project(7)[:, 32 - LATE :, :])):
        late_out[pair * LATE : (pair + 1) * LATE, :] = side.astype(BF16)
    for dz in far_first:
        go(late_copy(dz))

    total = packed[z]
    for dz in (1, 7, 2, 6, 3, 5, 4):
        sum_copy(dz).wait_recv()
        total = total + sums[dz - 1]
    shrunk[z] = jnp.concatenate([total, jnp.zeros((PADDED - PIECE, 128), F32)], axis=0).astype(BF16)

    def all_copy(dz):
        return remote(
            shrunk.at[z], shrunk.at[z], all_send.at[dz - 1], all_recv.at[dz - 1], dz=dz
        )

    def all_arrival(dz):
        k = lax.rem(z + (Z - dz), Z)
        return remote(
            shrunk.at[k], shrunk.at[k], all_send.at[dz - 1], all_recv.at[dz - 1], dz=dz
        )

    for dz in far_first:
        go(all_copy(dz))
    for way in range(2):
        for half in range(2):
            ring_copy(way, 4, half).wait_recv()
            span = slice(half * HALF, (half + 1) * HALF)
            part[0, span, :] += ring_in[way, 3, half].astype(F32)
    late = late_out[...].astype(F32)
    for dz in (1, 7, 2, 6, 3, 5, 4):
        late_copy(dz).wait_recv()
        late = late + late_in[dz - 1].astype(F32)
    late = late.astype(BF16).astype(F32)
    for dy in (1, 7, 2, 6, 3, 5, 4):
        up_copy(dy).wait_recv()
    go(remote(up.at[c], up.at[c], up_send.at[7], up_recv.at[7], dc=1))
    for dz in (1, 7, 2, 6, 3, 5, 4):
        all_arrival(dz).wait_recv()
    remote(up.at[1 - c], up.at[1 - c], up_send.at[7], up_recv.at[7], dc=1).wait_recv()

    low = iota((BLOCK, 128), 1) < RANK
    for pair in range(2):
        whole = shrunk[4 * pair : 4 * pair + 4].astype(F32)[:, :PIECE, :].reshape(BLOCK, 128)
        nearer = jnp.zeros((BLOCK - LATE, 128), F32)
        whole = whole + jnp.concatenate(
            [nearer, late[pair * LATE : (pair + 1) * LATE, :]], axis=0
        )
        swapped = jnp.concatenate([whole[:, RANK:], whole[:, :RANK]], axis=1)
        acc[2 * pair] = jnp.where(low, whole, swapped) * sel[2 * pair]
        acc[2 * pair + 1] = jnp.where(low, swapped, whole) * sel[2 * pair + 1]
    delta[...] = jnp.zeros(delta.shape, F32)
    for p in range(8):
        lo = window(p)
        mine = acc[:, lo : lo + 32, :]
        first, second = core_masks(p)
        wide = jnp.concatenate([mine * first, mine * second], axis=2).astype(BF16)
        maps = up[:, OFFSETS[p]].reshape(CORES * HELD, OUT)
        got = dot(wide.reshape(X * 32, 256), maps).reshape(X, 32, OUT)
        delta[:, lo : lo + 32, :] += got

    def back_copy(dx):
        return remote(
            back_out.at[dx - 1], back.at[dx], back_send.at[dx - 1], back_recv.at[dx - 1], dx=-dx
        )

    for dx in (2, 1, 3, 0):
        block = delta[dx]
        block = (adapter_scale * block).astype(BF16)
        if dx:
            back_out[dx - 1] = block
            back_copy(dx).start()
        else:
            back[0] = block
    started.extend(slow)
    settle()
    for dx in (1, 3, 2):
        back_copy(dx).wait_recv()
    mine = dot(perm_t[...], back[...].reshape(ALL, OUT))
    out_ref[...] = (part[0] + mine).astype(BF16)

    for dx in range(1, X):
        back_copy(dx).wait_send()


def local(
    tokens,
    token_adapter_index,
    adapter_stored_row,
    value_base_weight,
    adapter_down_maps,
    adapter_up_maps,
):
    vmem = pl.BlockSpec(memory_space=pltpu.VMEM)
    hbm = pl.BlockSpec(memory_space=pltpu.HBM)
    dma = pltpu.SemaphoreType.DMA
    return pl.pallas_call(
        kernel,
        out_shape=jax.ShapeDtypeStruct((ROWS, OUT), BF16),
        in_specs=[hbm] * 6,
        out_specs=vmem,
        scratch_shapes=[
            pltpu.VMEM((1, ROWS), I32),
            pltpu.VMEM((1, 2 * Y * X * CORES), I32),
            pltpu.VMEM((ROWS, WIDTH), BF16),
            pltpu.VMEM((WIDTH, Z * OUT), BF16),
            pltpu.VMEM((Y, CORES, HELD, WIDTH), BF16),
            pltpu.VMEM((CORES, Y, HELD, OUT), BF16),
            pltpu.VMEM((ALL + 128, ROWS), BF16),
            pltpu.VMEM((ROWS, ALL), BF16),
            pltpu.VMEM((X - 1, BLOCK, WIDTH), BF16),
            pltpu.VMEM((X, BLOCK, WIDTH), BF16),
            pltpu.VMEM((X - 1, 16, 256), BF16),
            pltpu.VMEM((X, 16, 256), BF16),
            pltpu.VMEM((Z, ROWS, OUT), F32),
            pltpu.VMEM((2, 4, 2, HALF, OUT), BF16),
            pltpu.VMEM((2, 4, 2, HALF, OUT), BF16),
            pltpu.VMEM((X, BLOCK, 128), F32),
            pltpu.VMEM((Z, PIECE, 128), F32),
            pltpu.VMEM((Z - 1, PIECE, 128), F32),
            pltpu.VMEM((Z, PADDED, 128), BF16),
            pltpu.VMEM((2 * LATE, 128), BF16),
            pltpu.VMEM((Z - 1, 2 * LATE, 128), BF16),
            pltpu.VMEM((X - 1, BLOCK, OUT), BF16),
            pltpu.VMEM((X, BLOCK, OUT), BF16),
            pltpu.VMEM((X, BLOCK, 128), F32),
            pltpu.VMEM((X, BLOCK, OUT), F32),
            dma((6,)),
            dma((2, 4, SUBS)),
            dma((2, 4, SUBS)),
            dma((Y + SUBS,)),
            dma((Y + SUBS,)),
            dma((Y,)),
            dma((Y,)),
            dma((2, X - 1)),
            dma((2, X - 1)),
            dma((2, 4, 2)),
            dma((2, 4, 2)),
            dma((Z - 1,)),
            dma((Z - 1,)),
            dma((Z - 1,)),
            dma((Z - 1,)),
            dma((Z - 1,)),
            dma((Z - 1,)),
            dma((X - 1,)),
            dma((X - 1,)),
        ],
        compiler_params=pltpu.CompilerParams(
            collective_id=0, has_side_effects=True, vmem_limit_bytes=60 << 20
        ),
        cost_estimate=pl.CostEstimate(
            flops=5_000_000_000, bytes_accessed=3_700_000, transcendentals=0
        ),
    )(
        token_adapter_index.reshape(1, ROWS),
        adapter_stored_row.reshape(1, -1),
        tokens,
        value_base_weight,
        adapter_down_maps.reshape(HELD, WIDTH),
        adapter_up_maps.reshape(HELD, OUT),
    )


def solution(mesh):
    return jax.shard_map(
        local,
        mesh=mesh,
        in_specs=(
            P("adapter", "tensor"),
            P("adapter"),
            P(),
            P("tensor", None),
            P("adapter", None, "tensor"),
            P("adapter", None, "tensor"),
        ),
        out_specs=P("adapter", "tensor"),
        check_vma=False,
    )
```

```python
import jax
import jax.numpy as jnp
from jax import lax
from jax.experimental import pallas as pl
from jax.experimental.pallas import tpu as pltpu
from jax.sharding import PartitionSpec as P

MESH = pl.DeviceIdType.MESH
BF16, F32, I32 = jnp.bfloat16, jnp.float32, jnp.int32

X, Y, CORES, Z = 4, 8, 2, 8
ROWS, WIDTH, OUT = 512, 1024, 128
CAP, RANK = 10, 64
FAR = Y // 2
LATE = 16
BLOCKS = X * CORES
BLOCK = Y * CAP
ALL = BLOCKS * BLOCK
SUBS = 4
HELD = 2 * RANK
SUB = HELD // SUBS
HALF = ROWS // 2
PIECE = BLOCK // 2
PADDED = 48
PAIRS = BLOCKS // 2
OFFSETS = (0, 1, 7, 2, 6, 3, 5, 4)
OTHERS = (2, 6, 3, 7, 4, 5, 1)
adapter_scale = 2.0


def dot(a, b):
    return jnp.dot(a, b, preferred_element_type=F32)


def dot_nt(a, b):
    return lax.dot_general(a, b, (((1,), (1,)), ((), ())), preferred_element_type=F32)


def iota(shape, axis):
    return lax.broadcasted_iota(I32, shape, axis)


def kernel(
    idx_hbm,
    stored_hbm,
    tok_hbm,
    w_hbm,
    down_hbm,
    up_hbm,
    out_ref,
    idx_ref,
    stored_ref,
    tok,
    w,
    down,
    up,
    perm,
    perm_t,
    send_rows,
    rows,
    send_place,
    place,
    part,
    ring_out,
    ring_in,
    acc,
    packed,
    sums,
    shrunk,
    late_out,
    late_in,
    back_out,
    back,
    sel,
    delta,
    local_sem,
    y_send,
    y_recv,
    up_send,
    up_recv,
    x_send,
    x_recv,
    ring_send,
    ring_recv,
    sum_send,
    sum_recv,
    all_send,
    all_recv,
    late_send,
    late_recv,
    back_send,
    back_recv,
):
    a = lax.axis_index("adapter")
    z = lax.axis_index("tensor")
    x, y, c = a // (Y * CORES), (a // CORES) % Y, a % CORES

    def device(dx=0, dy=0, dc=0, dz=0):
        ax = lax.rem(x + (dx + X), X)
        ay = lax.rem(y + (dy + Y), Y)
        ac = lax.rem(c + dc, CORES)
        return ((ax * Y + ay) * CORES + ac, lax.rem(z + (dz + Z), Z))

    def remote(src, dst, send, recv, **to):
        return pltpu.make_async_remote_copy(
            src_ref=src,
            dst_ref=dst,
            send_sem=send,
            recv_sem=recv,
            device_id=device(**to),
            device_id_type=MESH,
        )

    started, slow = [], []

    def go(copy):
        copy.start()
        started.append(copy)

    barrier = pltpu.get_barrier_semaphore()
    partners = [dict(dx=b // 2, dc=b % 2) for b in OTHERS]
    partners += [dict(dy=d) for d in range(1, Y)]
    partners += [dict(dz=d) for d in range(1, Z)]
    for to in partners:
        pl.semaphore_signal(barrier, inc=1, device_id=device(**to), device_id_type=MESH)
    load_idx = pltpu.make_async_copy(idx_hbm, idx_ref, local_sem.at[4])
    load_stored = pltpu.make_async_copy(stored_hbm, stored_ref, local_sem.at[5])
    load_down = pltpu.make_async_copy(down_hbm, down.at[0], local_sem.at[0])
    load_tok = pltpu.make_async_copy(tok_hbm, tok, local_sem.at[1])
    load_w = pltpu.make_async_copy(w_hbm, w, local_sem.at[2])
    load_up = pltpu.make_async_copy(up_hbm, up.at[0], local_sem.at[3])
    for load in (load_down, load_idx, load_stored, load_tok, load_up, load_w):
        load.start()

    def y_slot(way, hop):
        return (Y - hop) % Y if way == 0 else hop

    def y_copy(way, hop, sub):
        span = pl.ds(sub * SUB, SUB)
        return remote(
            down.at[y_slot(way, hop - 1), span],
            down.at[y_slot(way, hop), span],
            y_send.at[way, hop - 1, sub],
            y_recv.at[way, hop - 1, sub],
            dy=1 if way == 0 else -1,
        )

    def y_subs(way, hop):
        first, last = range(SUBS // 2), range(SUBS // 2, SUBS)
        order = (*first, *last) if way == 0 else (*last, *first)
        return order[: SUBS // 2] if hop == Y // 2 else order

    load_down.wait()
    pl.semaphore_wait(barrier, len(partners))
    for i in range(SUBS):
        for way in range(2):
            go(y_copy(way, 1, y_subs(way, 1)[i]))

    def piece_copy(slot, sub, core):
        span = pl.ds(sub * SUB, SUB)
        place = Y + PIECEWISE.index(slot) * SUBS + sub
        return remote(
            down.at[slot, core, span],
            down.at[slot, core, span],
            core_send.at[place],
            core_recv.at[place],
            dc=1,
        )

    load_idx.wait()
    load_stored.wait()
    idx = idx_ref[...]
    stored = jnp.broadcast_to(stored_ref[...].astype(F32), (8, 128)).astype(BF16)
    lookup = jnp.where(iota((128, ROWS), 0) == idx, 1.0, 0.0).astype(BF16)
    slot = dot(stored, lookup)[0:1].astype(I32)
    owner = slot // 2
    within = slot - owner * 2
    member = jnp.where(iota((64, ROWS), 0) == owner, 1.0, 0.0)
    earlier = jnp.where(iota((ROWS, ROWS), 0) < iota((ROWS, ROWS), 1), 1.0, 0.0).astype(BF16)
    before = jnp.sum(dot(member.astype(BF16), earlier) * member, axis=0, keepdims=True)
    owner_x, owner_y, owner_c = owner // 16, (owner // 2) & 7, owner & 1
    step_x = (owner_x - x) & 3
    step_y = (owner_y - y) & 7
    position = jnp.where(
        step_y == 0, 0, jnp.where(step_y <= 4, 2 * step_y - 1, 2 * (8 - step_y))
    )
    block_of = step_x * CORES + ((owner_c - c) & 1)
    target = block_of * BLOCK + position * CAP + before.astype(I32)
    perm[...] = jnp.where(iota((ALL + 128, ROWS), 0) == target, 1.0, 0.0).astype(BF16)
    within16 = jnp.broadcast_to(within.astype(F32), (16, ROWS)).astype(BF16)

    def x_copies(b):
        to = dict(dx=b // 2, dc=b % 2)
        return (
            remote(send_rows.at[b - 1], rows.at[b], x_send.at[0, b - 1], x_recv.at[0, b - 1], **to),
            remote(
                send_place.at[b - 1], place.at[b], x_send.at[1, b - 1], x_recv.at[1, b - 1], **to
            ),
        )

    load_tok.wait()
    for b in (*OTHERS, 0):
        block = dot(perm[b * BLOCK : (b + 1) * BLOCK, :], tok[...]).astype(BF16)
        where = dot_nt(within16, perm[b * BLOCK : b * BLOCK + 128, :]).astype(BF16)
        if b:
            send_rows[b - 1] = block
            send_place[b - 1] = where
            for copy in x_copies(b):
                copy.start()
                slow.append(copy)
        else:
            rows[0] = block
            place[0] = where

    def product(m):
        k = lax.rem(z + m, Z)
        part[m] = dot(tok[...], w[:, pl.ds(pl.multiple_of(k * OUT, OUT), OUT)])

    def ring_copy(way, step, half):
        return remote(
            ring_out.at[way, step - 1, half],
            ring_in.at[way, step - 1, half],
            ring_send.at[way, step - 1, half],
            ring_recv.at[way, step - 1, half],
            dz=1 if way == 0 else -1,
        )

    def ring_m(way, step):
        return 5 - step if way == 0 else 3 + step

    def ring_pass(way, step, half, arrived):
        m = ring_m(way, step)
        value = part[m, half * HALF : (half + 1) * HALF, :]
        if arrived:
            ring_copy(way, step - 1, half).wait_recv()
            value = value + ring_in[way, step - 2, half].astype(F32)
        ring_out[way, step - 1, half] = value.astype(BF16)
        go(ring_copy(way, step, half))

    load_up.wait()
    load_w.wait()
    def y_forward(hop, i):
        for way in range(2):
            sub = y_subs(way, hop)[i]
            y_copy(way, hop, sub).wait_recv()
            if hop < FAR and sub in y_subs(way, hop + 1):
                go(y_copy(way, hop + 1, sub))

    def ring_step(step):
        for way in range(2):
            first = way
            halves = (first,) if step == 1 else (first, 1 - first)
            for half in halves:
                ring_pass(way, step + 1, half, True)

    def settle():
        while started:
            started.pop(0).wait_send()

    product(4)
    for way in range(2):
        ring_pass(way, 1, way, False)
    product(3)
    ring_pass(0, 2, 1, False)
    product(5)
    ring_pass(1, 2, 0, False)
    y_forward(1, 0)
    product(2)
    product(6)
    y_forward(1, 1)
    product(1)
    product(7)
    y_forward(1, 2)
    ring_step(1)
    y_forward(1, 3)
    product(0)
    perm_t[...] = jnp.transpose(perm[0:ALL, :])
    y_forward(2, 0)
    y_forward(2, 1)
    ring_step(2)
    y_forward(2, 2)
    y_forward(2, 3)
    y_forward(3, 0)
    ring_step(3)
    y_forward(3, 1)
    y_forward(3, 2)
    y_forward(3, 3)
    recent = started[-10:]
    del started[-10:]
    settle()
    started.extend(recent)

    def up_copy(dy):
        return remote(
            up.at[0], up.at[Y - dy], up_send.at[dy - 1], up_recv.at[dy - 1], dy=dy
        )


    acc[...] = jnp.zeros(acc.shape, F32)
    eye = iota((BLOCK, 128), 0) == iota((BLOCK, 128), 1)
    ones = jnp.ones((128, 128), BF16)
    for b in (0, *OTHERS):
        if b:
            for copy in x_copies(b):
                copy.wait_recv()
        spread = jnp.where(eye, place[b, 0:1, :].astype(F32), 0.0).astype(BF16)
        sel[b] = jnp.where(
            dot(spread, ones).astype(I32) == iota((BLOCK, 128), 1) // RANK, 1.0, 0.0
        )

    def window(p):
        return min((p * CAP) // 16 * 16, BLOCK - 32)

    def kept_rows(p):
        row = window(p) + iota((BLOCKS, 32, 128), 1) - p * CAP
        return jnp.where((row >= 0) & (row < CAP), 1.0, 0.0) * sel[:, window(p) : window(p) + 32, :]

    def down_project(p):
        lo = window(p)
        mine = rows[:, lo : lo + 32, :].reshape(BLOCKS * 32, WIDTH)
        return dot_nt(mine, down[OFFSETS[p]]).reshape(BLOCKS, 32, 128) * kept_rows(p)

    for p in range(7):
        lo = window(p)
        acc[:, lo : lo + 32, :] += down_project(p)

    def side_by_side(found):
        whole = found + jnp.concatenate([found[:, :, RANK:], found[:, :, :RANK]], axis=2)
        low = iota(whole.shape[1:], 1) < RANK
        return [jnp.where(low, whole[2 * pair], whole[2 * pair + 1]) for pair in range(PAIRS)]

    for pair, side in enumerate(side_by_side(acc[...])):
        side = side.reshape(2, PIECE, 128)
        side = jnp.concatenate([side, jnp.zeros((2, PADDED - PIECE, 128), F32)], axis=1)
        packed[2 * pair : 2 * pair + 2] = side.astype(BF16)

    def sum_copy(dz):
        return remote(
            packed.at[lax.rem(z + dz, Z)],
            sums.at[dz - 1],
            sum_send.at[dz - 1],
            sum_recv.at[dz - 1],
            dz=dz,
        )

    far_first = (4, 3, 5, 2, 6, 1, 7)
    for dz in far_first:
        go(sum_copy(dz))
    def late_copy(dz):
        return remote(
            late_out, late_in.at[dz - 1], late_send.at[dz - 1], late_recv.at[dz - 1], dz=dz
        )

    for i in range(SUBS // 2):
        y_forward(FAR, i)
    for dy in far_first:
        go(up_copy(dy))
    for pair, side in enumerate(side_by_side(down_project(7)[:, 32 - LATE :, :])):
        late_out[pair * LATE : (pair + 1) * LATE, :] = side.astype(BF16)
    for dz in far_first:
        go(late_copy(dz))

    total = packed[z].astype(F32)
    for dz in (1, 7, 2, 6, 3, 5, 4):
        sum_copy(dz).wait_recv()
        total = total + sums[dz - 1].astype(F32)
    shrunk[z] = total.astype(BF16)

    def all_copy(dz):
        return remote(
            shrunk.at[z], shrunk.at[z], all_send.at[dz - 1], all_recv.at[dz - 1], dz=dz
        )

    def all_arrival(dz):
        k = lax.rem(z + (Z - dz), Z)
        return remote(
            shrunk.at[k], shrunk.at[k], all_send.at[dz - 1], all_recv.at[dz - 1], dz=dz
        )

    for dz in far_first:
        go(all_copy(dz))
    for way in range(2):
        for half in range(2):
            ring_copy(way, 4, half).wait_recv()
            span = slice(half * HALF, (half + 1) * HALF)
            part[0, span, :] += ring_in[way, 3, half].astype(F32)
    late = late_out[...].astype(F32)
    for dz in (1, 7, 2, 6, 3, 5, 4):
        late_copy(dz).wait_recv()
        late = late + late_in[dz - 1].astype(F32)
    late = late.astype(BF16).astype(F32)
    for dy in (1, 7, 2, 6, 3, 5, 4):
        up_copy(dy).wait_recv()
    for dz in (1, 7, 2, 6, 3, 5, 4):
        all_arrival(dz).wait_recv()

    low = iota((BLOCK, 128), 1) < RANK
    for pair in range(PAIRS):
        whole = shrunk[2 * pair : 2 * pair + 2].astype(F32)[:, :PIECE, :].reshape(BLOCK, 128)
        nearer = jnp.zeros((BLOCK - LATE, 128), F32)
        whole = whole + jnp.concatenate(
            [nearer, late[pair * LATE : (pair + 1) * LATE, :]], axis=0
        )
        swapped = jnp.concatenate([whole[:, RANK:], whole[:, :RANK]], axis=1)
        acc[2 * pair] = jnp.where(low, whole, swapped) * sel[2 * pair]
        acc[2 * pair + 1] = jnp.where(low, swapped, whole) * sel[2 * pair + 1]
    delta[...] = jnp.zeros(delta.shape, F32)
    for p in range(8):
        lo = window(p)
        mine = (acc[:, lo : lo + 32, :] * kept_rows(p)).astype(BF16)
        got = dot(mine.reshape(BLOCKS * 32, 128), up[OFFSETS[p]])
        delta[:, lo : lo + 32, :] += got.reshape(BLOCKS, 32, OUT)

    def back_copy(b):
        return remote(
            back_out.at[b - 1],
            back.at[b],
            back_send.at[b - 1],
            back_recv.at[b - 1],
            dx=-(b // 2),
            dc=b % 2,
        )

    for b in (5, 4, 7, 3, 6, 2, 1, 0):
        block = (adapter_scale * delta[b]).astype(BF16)
        if b:
            back_out[b - 1] = block
            back_copy(b).start()
        else:
            back[0] = block
    started.extend(slow)
    settle()
    for b in OTHERS:
        back_copy(b).wait_recv()
    mine = dot(perm_t[...], back[...].reshape(ALL, OUT))
    out_ref[...] = (part[0] + mine).astype(BF16)

    for b in OTHERS:
        back_copy(b).wait_send()


def local(
    tokens,
    token_adapter_index,
    adapter_stored_row,
    value_base_weight,
    adapter_down_maps,
    adapter_up_maps,
):
    vmem = pl.BlockSpec(memory_space=pltpu.VMEM)
    hbm = pl.BlockSpec(memory_space=pltpu.HBM)
    dma = pltpu.SemaphoreType.DMA
    return pl.pallas_call(
        kernel,
        out_shape=jax.ShapeDtypeStruct((ROWS, OUT), BF16),
        in_specs=[hbm] * 6,
        out_specs=vmem,
        scratch_shapes=[
            pltpu.VMEM((1, ROWS), I32),
            pltpu.VMEM((1, 2 * Y * X * CORES), I32),
            pltpu.VMEM((ROWS, WIDTH), BF16),
            pltpu.VMEM((WIDTH, Z * OUT), BF16),
            pltpu.VMEM((Y, HELD, WIDTH), BF16),
            pltpu.VMEM((Y, HELD, OUT), BF16),
            pltpu.VMEM((ALL + 128, ROWS), BF16),
            pltpu.VMEM((ROWS, ALL), BF16),
            pltpu.VMEM((BLOCKS - 1, BLOCK, WIDTH), BF16),
            pltpu.VMEM((BLOCKS, BLOCK, WIDTH), BF16),
            pltpu.VMEM((BLOCKS - 1, 16, 128), BF16),
            pltpu.VMEM((BLOCKS, 16, 128), BF16),
            pltpu.VMEM((Z, ROWS, OUT), F32),
            pltpu.VMEM((2, 4, 2, HALF, OUT), BF16),
            pltpu.VMEM((2, 4, 2, HALF, OUT), BF16),
            pltpu.VMEM((BLOCKS, BLOCK, 128), F32),
            pltpu.VMEM((Z, PADDED, 128), BF16),
            pltpu.VMEM((Z - 1, PADDED, 128), BF16),
            pltpu.VMEM((Z, PADDED, 128), BF16),
            pltpu.VMEM((PAIRS * LATE, 128), BF16),
            pltpu.VMEM((Z - 1, PAIRS * LATE, 128), BF16),
            pltpu.VMEM((BLOCKS - 1, BLOCK, OUT), BF16),
            pltpu.VMEM((BLOCKS, BLOCK, OUT), BF16),
            pltpu.VMEM((BLOCKS, BLOCK, 128), F32),
            pltpu.VMEM((BLOCKS, BLOCK, OUT), F32),
            dma((6,)),
            dma((2, 4, SUBS)),
            dma((2, 4, SUBS)),
            dma((Y,)),
            dma((Y,)),
            dma((2, BLOCKS - 1)),
            dma((2, BLOCKS - 1)),
            dma((2, 4, 2)),
            dma((2, 4, 2)),
            dma((Z - 1,)),
            dma((Z - 1,)),
            dma((Z - 1,)),
            dma((Z - 1,)),
            dma((Z - 1,)),
            dma((Z - 1,)),
            dma((BLOCKS - 1,)),
            dma((BLOCKS - 1,)),
        ],
        compiler_params=pltpu.CompilerParams(
            collective_id=0, has_side_effects=True, vmem_limit_bytes=60 << 20
        ),
        cost_estimate=pl.CostEstimate(
            flops=5_000_000_000, bytes_accessed=3_700_000, transcendentals=0
        ),
    )(
        token_adapter_index.reshape(1, ROWS),
        adapter_stored_row.reshape(1, -1),
        tokens,
        value_base_weight,
        adapter_down_maps.reshape(HELD, WIDTH),
        adapter_up_maps.reshape(HELD, OUT),
    )


def solution(mesh):
    return jax.shard_map(
        local,
        mesh=mesh,
        in_specs=(
            P("adapter", "tensor"),
            P("adapter"),
            P(),
            P("tensor", None),
            P("adapter", None, "tensor"),
            P("adapter", None, "tensor"),
        ),
        out_specs=P("adapter", "tensor"),
        check_vma=False,
    )
```

```python
import jax
import jax.numpy as jnp
from jax import lax
from jax.experimental import pallas as pl
from jax.experimental.pallas import tpu as pltpu
from jax.sharding import PartitionSpec as P

MESH = pl.DeviceIdType.MESH
BF16, F32, I32 = jnp.bfloat16, jnp.float32, jnp.int32

X, Y, CORES, Z = 4, 8, 2, 8
ROWS, WIDTH, OUT = 512, 1024, 128
CAP, RANK = 10, 64
FAR = Y // 2
LATE = 16
BLOCKS = X * CORES
BLOCK = Y * CAP
ALL = BLOCKS * BLOCK
SUBS = 4
HELD = 2 * RANK
SUB = HELD // SUBS
HALF = ROWS // 2
PIECE = BLOCK // 2
PADDED = 48
PAIRS = BLOCKS // 2
OFFSETS = (0, 1, 7, 2, 6, 3, 5, 4)
OTHERS = (2, 6, 3, 7, 4, 5, 1)
adapter_scale = 2.0


def dot(a, b):
    return jnp.dot(a, b, preferred_element_type=F32)


def dot_nt(a, b):
    return lax.dot_general(a, b, (((1,), (1,)), ((), ())), preferred_element_type=F32)


def iota(shape, axis):
    return lax.broadcasted_iota(I32, shape, axis)


def kernel(
    idx_hbm,
    stored_hbm,
    tok_hbm,
    w_hbm,
    down_hbm,
    up_hbm,
    out_ref,
    idx_ref,
    stored_ref,
    tok,
    w,
    down,
    up,
    perm,
    perm_t,
    send_rows,
    rows,
    send_place,
    place,
    part,
    ring_out,
    ring_in,
    acc,
    packed,
    sums,
    shrunk,
    late_out,
    late_in,
    back_out,
    back,
    sel,
    delta,
    local_sem,
    y_send,
    y_recv,
    up_send,
    up_recv,
    x_send,
    x_recv,
    ring_send,
    ring_recv,
    sum_send,
    sum_recv,
    all_send,
    all_recv,
    late_send,
    late_recv,
    back_send,
    back_recv,
):
    a = lax.axis_index("adapter")
    z = lax.axis_index("tensor")
    x, y, c = a // (Y * CORES), (a // CORES) % Y, a % CORES

    def device(dx=0, dy=0, dc=0, dz=0):
        ax = lax.rem(x + (dx + X), X)
        ay = lax.rem(y + (dy + Y), Y)
        ac = lax.rem(c + dc, CORES)
        return ((ax * Y + ay) * CORES + ac, lax.rem(z + (dz + Z), Z))

    def remote(src, dst, send, recv, **to):
        return pltpu.make_async_remote_copy(
            src_ref=src,
            dst_ref=dst,
            send_sem=send,
            recv_sem=recv,
            device_id=device(**to),
            device_id_type=MESH,
        )

    started, slow = [], []

    def go(copy):
        copy.start()
        started.append(copy)

    barrier = pltpu.get_barrier_semaphore()
    partners = [dict(dx=b // 2, dc=b % 2) for b in OTHERS]
    partners += [dict(dy=d) for d in range(1, Y)]
    partners += [dict(dz=d) for d in range(1, Z)]
    for to in partners:
        pl.semaphore_signal(barrier, inc=1, device_id=device(**to), device_id_type=MESH)
    load_idx = pltpu.make_async_copy(idx_hbm, idx_ref, local_sem.at[4])
    load_stored = pltpu.make_async_copy(stored_hbm, stored_ref, local_sem.at[5])
    load_down = pltpu.make_async_copy(down_hbm, down.at[0], local_sem.at[0])
    load_tok = pltpu.make_async_copy(tok_hbm, tok, local_sem.at[1])
    load_w = pltpu.make_async_copy(w_hbm, w, local_sem.at[2])
    load_up = pltpu.make_async_copy(up_hbm, up.at[0], local_sem.at[3])
    for load in (load_down, load_idx, load_stored, load_tok, load_up, load_w):
        load.start()

    def y_slot(way, hop):
        return (Y - hop) % Y if way == 0 else hop

    def y_copy(way, hop, sub):
        span = pl.ds(sub * SUB, SUB)
        return remote(
            down.at[y_slot(way, hop - 1), span],
            down.at[y_slot(way, hop), span],
            y_send.at[way, hop - 1, sub],
            y_recv.at[way, hop - 1, sub],
            dy=1 if way == 0 else -1,
        )

    def y_subs(way, hop):
        first, last = range(SUBS // 2), range(SUBS // 2, SUBS)
        order = (*first, *last) if way == 0 else (*last, *first)
        return order[: SUBS // 2] if hop == Y // 2 else order

    load_down.wait()
    pl.semaphore_wait(barrier, len(partners))
    for i in range(SUBS):
        for way in range(2):
            go(y_copy(way, 1, y_subs(way, 1)[i]))

    def piece_copy(slot, sub, core):
        span = pl.ds(sub * SUB, SUB)
        place = Y + PIECEWISE.index(slot) * SUBS + sub
        return remote(
            down.at[slot, core, span],
            down.at[slot, core, span],
            core_send.at[place],
            core_recv.at[place],
            dc=1,
        )

    load_idx.wait()
    load_stored.wait()
    idx = idx_ref[...]
    stored = jnp.broadcast_to(stored_ref[...].astype(F32), (8, 128)).astype(BF16)
    lookup = jnp.where(iota((128, ROWS), 0) == idx, 1.0, 0.0).astype(BF16)
    slot = dot(stored, lookup)[0:1].astype(I32)
    owner = slot // 2
    within = slot - owner * 2
    member = jnp.where(iota((64, ROWS), 0) == owner, 1.0, 0.0)
    earlier = jnp.where(iota((ROWS, ROWS), 0) < iota((ROWS, ROWS), 1), 1.0, 0.0).astype(BF16)
    before = jnp.sum(dot(member.astype(BF16), earlier) * member, axis=0, keepdims=True)
    owner_x, owner_y, owner_c = owner // 16, (owner // 2) & 7, owner & 1
    step_x = (owner_x - x) & 3
    step_y = (owner_y - y) & 7
    position = jnp.where(
        step_y == 0, 0, jnp.where(step_y <= 4, 2 * step_y - 1, 2 * (8 - step_y))
    )
    block_of = step_x * CORES + ((owner_c - c) & 1)
    target = block_of * BLOCK + position * CAP + before.astype(I32)
    perm[...] = jnp.where(iota((ALL + 128, ROWS), 0) == target, 1.0, 0.0).astype(BF16)
    within16 = jnp.broadcast_to(within.astype(F32), (16, ROWS)).astype(BF16)

    def x_copies(b):
        to = dict(dx=b // 2, dc=b % 2)
        return (
            remote(send_rows.at[b - 1], rows.at[b], x_send.at[0, b - 1], x_recv.at[0, b - 1], **to),
            remote(
                send_place.at[b - 1], place.at[b], x_send.at[1, b - 1], x_recv.at[1, b - 1], **to
            ),
        )

    load_tok.wait()
    for dx in (1, 3, 2, 0):
        pair = dot(perm[2 * dx * BLOCK : (2 * dx + 2) * BLOCK, :], tok[...]).astype(BF16)
        for b in (2 * dx, 2 * dx + 1):
            block = pair[(b - 2 * dx) * BLOCK : (b - 2 * dx + 1) * BLOCK]
            where = dot_nt(within16, perm[b * BLOCK : b * BLOCK + 128, :]).astype(BF16)
            if b:
                send_rows[b - 1] = block
                send_place[b - 1] = where
                for copy in x_copies(b):
                    copy.start()
                    slow.append(copy)
            else:
                rows[0] = block
                place[0] = where

    def product(m):
        k = lax.rem(z + m, Z)
        part[m] = dot(tok[...], w[:, pl.ds(pl.multiple_of(k * OUT, OUT), OUT)])

    def ring_copy(way, step, half):
        return remote(
            ring_out.at[way, step - 1, half],
            ring_in.at[way, step - 1, half],
            ring_send.at[way, step - 1, half],
            ring_recv.at[way, step - 1, half],
            dz=1 if way == 0 else -1,
        )

    def ring_m(way, step):
        return 5 - step if way == 0 else 3 + step

    def ring_pass(way, step, half, arrived):
        m = ring_m(way, step)
        value = part[m, half * HALF : (half + 1) * HALF, :]
        if arrived:
            ring_copy(way, step - 1, half).wait_recv()
            value = value + ring_in[way, step - 2, half].astype(F32)
        ring_out[way, step - 1, half] = value.astype(BF16)
        go(ring_copy(way, step, half))

    load_up.wait()
    load_w.wait()
    def y_forward(hop, i):
        for way in range(2):
            sub = y_subs(way, hop)[i]
            y_copy(way, hop, sub).wait_recv()
            if hop < FAR and sub in y_subs(way, hop + 1):
                go(y_copy(way, hop + 1, sub))

    def ring_step(step):
        for way in range(2):
            first = way
            halves = (first,) if step == 1 else (first, 1 - first)
            for half in halves:
                ring_pass(way, step + 1, half, True)

    def settle():
        while started:
            started.pop(0).wait_send()

    product(4)
    for way in range(2):
        ring_pass(way, 1, way, False)
    product(3)
    ring_pass(0, 2, 1, False)
    product(5)
    ring_pass(1, 2, 0, False)
    y_forward(1, 0)
    product(2)
    product(6)
    y_forward(1, 1)
    product(1)
    product(7)
    y_forward(1, 2)
    ring_step(1)
    y_forward(1, 3)
    product(0)
    perm_t[...] = jnp.transpose(perm[0:ALL, :])
    y_forward(2, 0)
    y_forward(2, 1)
    ring_step(2)
    y_forward(2, 2)
    y_forward(2, 3)
    y_forward(3, 0)
    ring_step(3)
    y_forward(3, 1)
    y_forward(3, 2)
    y_forward(3, 3)
    recent = started[-10:]
    del started[-10:]
    settle()
    started.extend(recent)

    def up_copy(dy):
        return remote(
            up.at[0], up.at[Y - dy], up_send.at[dy - 1], up_recv.at[dy - 1], dy=dy
        )


    acc[...] = jnp.zeros(acc.shape, F32)
    eye = iota((BLOCK, 128), 0) == iota((BLOCK, 128), 1)
    ones = jnp.ones((128, 128), BF16)
    for b in (0, *OTHERS):
        if b:
            for copy in x_copies(b):
                copy.wait_recv()
        spread = jnp.where(eye, place[b, 0:1, :].astype(F32), 0.0).astype(BF16)
        sel[b] = jnp.where(
            dot(spread, ones).astype(I32) == iota((BLOCK, 128), 1) // RANK, 1.0, 0.0
        )

    def window(p):
        return min((p * CAP) // 16 * 16, BLOCK - 32)

    def kept_rows(p):
        row = window(p) + iota((BLOCKS, 32, 128), 1) - p * CAP
        return jnp.where((row >= 0) & (row < CAP), 1.0, 0.0) * sel[:, window(p) : window(p) + 32, :]

    def down_project(p):
        lo = window(p)
        mine = rows[:, lo : lo + 32, :].reshape(BLOCKS * 32, WIDTH)
        return dot_nt(mine, down[OFFSETS[p]]).reshape(BLOCKS, 32, 128) * kept_rows(p)

    for p in range(7):
        lo = window(p)
        acc[:, lo : lo + 32, :] += down_project(p)

    def side_by_side(found):
        whole = found + jnp.concatenate([found[:, :, RANK:], found[:, :, :RANK]], axis=2)
        low = iota(whole.shape[1:], 1) < RANK
        return [jnp.where(low, whole[2 * pair], whole[2 * pair + 1]) for pair in range(PAIRS)]

    for pair, side in enumerate(side_by_side(acc[...])):
        side = side.reshape(2, PIECE, 128)
        side = jnp.concatenate([side, jnp.zeros((2, PADDED - PIECE, 128), F32)], axis=1)
        packed[2 * pair : 2 * pair + 2] = side.astype(BF16)

    def sum_copy(dz):
        return remote(
            packed.at[lax.rem(z + dz, Z)],
            sums.at[dz - 1],
            sum_send.at[dz - 1],
            sum_recv.at[dz - 1],
            dz=dz,
        )

    far_first = (4, 3, 5, 2, 6, 1, 7)
    for dz in far_first:
        go(sum_copy(dz))
    def late_copy(dz):
        return remote(
            late_out, late_in.at[dz - 1], late_send.at[dz - 1], late_recv.at[dz - 1], dz=dz
        )

    for i in range(SUBS // 2):
        y_forward(FAR, i)
    for dy in far_first:
        go(up_copy(dy))
    for pair, side in enumerate(side_by_side(down_project(7)[:, 32 - LATE :, :])):
        late_out[pair * LATE : (pair + 1) * LATE, :] = side.astype(BF16)
    for dz in far_first:
        go(late_copy(dz))

    total = packed[z].astype(F32)
    for dz in (1, 7, 2, 6, 3, 5, 4):
        sum_copy(dz).wait_recv()
        total = total + sums[dz - 1].astype(F32)
    shrunk[z] = total.astype(BF16)

    def all_copy(dz):
        return remote(
            shrunk.at[z], shrunk.at[z], all_send.at[dz - 1], all_recv.at[dz - 1], dz=dz
        )

    def all_arrival(dz):
        k = lax.rem(z + (Z - dz), Z)
        return remote(
            shrunk.at[k], shrunk.at[k], all_send.at[dz - 1], all_recv.at[dz - 1], dz=dz
        )

    for dz in far_first:
        go(all_copy(dz))
    for way in range(2):
        for half in range(2):
            ring_copy(way, 4, half).wait_recv()
            span = slice(half * HALF, (half + 1) * HALF)
            part[0, span, :] += ring_in[way, 3, half].astype(F32)
    late = late_out[...].astype(F32)
    for dz in (1, 7, 2, 6, 3, 5, 4):
        late_copy(dz).wait_recv()
        late = late + late_in[dz - 1].astype(F32)
    late = late.astype(BF16).astype(F32)
    for dy in (1, 7, 2, 6, 3, 5, 4):
        up_copy(dy).wait_recv()
    for dz in (1, 7, 2, 6, 3, 5, 4):
        all_arrival(dz).wait_recv()

    low = iota((BLOCK, 128), 1) < RANK
    for pair in range(PAIRS):
        whole = shrunk[2 * pair : 2 * pair + 2].astype(F32)[:, :PIECE, :].reshape(BLOCK, 128)
        nearer = jnp.zeros((BLOCK - LATE, 128), F32)
        whole = whole + jnp.concatenate(
            [nearer, late[pair * LATE : (pair + 1) * LATE, :]], axis=0
        )
        swapped = jnp.concatenate([whole[:, RANK:], whole[:, :RANK]], axis=1)
        acc[2 * pair] = jnp.where(low, whole, swapped) * sel[2 * pair]
        acc[2 * pair + 1] = jnp.where(low, swapped, whole) * sel[2 * pair + 1]
    delta[...] = jnp.zeros(delta.shape, F32)
    for p in range(8):
        lo = window(p)
        mine = (acc[:, lo : lo + 32, :] * kept_rows(p)).astype(BF16)
        got = dot(mine.reshape(BLOCKS * 32, 128), up[OFFSETS[p]])
        delta[:, lo : lo + 32, :] += got.reshape(BLOCKS, 32, OUT)

    def back_copy(b):
        return remote(
            back_out.at[b - 1],
            back.at[b],
            back_send.at[b - 1],
            back_recv.at[b - 1],
            dx=-(b // 2),
            dc=b % 2,
        )

    for b in (5, 4, 7, 3, 6, 2, 1, 0):
        block = (adapter_scale * delta[b]).astype(BF16)
        if b:
            back_out[b - 1] = block
            back_copy(b).start()
        else:
            back[0] = block
    started.extend(slow)
    settle()
    for b in OTHERS:
        back_copy(b).wait_recv()
    mine = dot(perm_t[...], back[...].reshape(ALL, OUT))
    out_ref[...] = (part[0] + mine).astype(BF16)

    for b in OTHERS:
        back_copy(b).wait_send()


def local(
    tokens,
    token_adapter_index,
    adapter_stored_row,
    value_base_weight,
    adapter_down_maps,
    adapter_up_maps,
):
    vmem = pl.BlockSpec(memory_space=pltpu.VMEM)
    hbm = pl.BlockSpec(memory_space=pltpu.HBM)
    dma = pltpu.SemaphoreType.DMA
    return pl.pallas_call(
        kernel,
        out_shape=jax.ShapeDtypeStruct((ROWS, OUT), BF16),
        in_specs=[hbm] * 6,
        out_specs=vmem,
        scratch_shapes=[
            pltpu.VMEM((1, ROWS), I32),
            pltpu.VMEM((1, 2 * Y * X * CORES), I32),
            pltpu.VMEM((ROWS, WIDTH), BF16),
            pltpu.VMEM((WIDTH, Z * OUT), BF16),
            pltpu.VMEM((Y, HELD, WIDTH), BF16),
            pltpu.VMEM((Y, HELD, OUT), BF16),
            pltpu.VMEM((ALL + 128, ROWS), BF16),
            pltpu.VMEM((ROWS, ALL), BF16),
            pltpu.VMEM((BLOCKS - 1, BLOCK, WIDTH), BF16),
            pltpu.VMEM((BLOCKS, BLOCK, WIDTH), BF16),
            pltpu.VMEM((BLOCKS - 1, 16, 128), BF16),
            pltpu.VMEM((BLOCKS, 16, 128), BF16),
            pltpu.VMEM((Z, ROWS, OUT), F32),
            pltpu.VMEM((2, 4, 2, HALF, OUT), BF16),
            pltpu.VMEM((2, 4, 2, HALF, OUT), BF16),
            pltpu.VMEM((BLOCKS, BLOCK, 128), F32),
            pltpu.VMEM((Z, PADDED, 128), BF16),
            pltpu.VMEM((Z - 1, PADDED, 128), BF16),
            pltpu.VMEM((Z, PADDED, 128), BF16),
            pltpu.VMEM((PAIRS * LATE, 128), BF16),
            pltpu.VMEM((Z - 1, PAIRS * LATE, 128), BF16),
            pltpu.VMEM((BLOCKS - 1, BLOCK, OUT), BF16),
            pltpu.VMEM((BLOCKS, BLOCK, OUT), BF16),
            pltpu.VMEM((BLOCKS, BLOCK, 128), F32),
            pltpu.VMEM((BLOCKS, BLOCK, OUT), F32),
            dma((6,)),
            dma((2, 4, SUBS)),
            dma((2, 4, SUBS)),
            dma((Y,)),
            dma((Y,)),
            dma((2, BLOCKS - 1)),
            dma((2, BLOCKS - 1)),
            dma((2, 4, 2)),
            dma((2, 4, 2)),
            dma((Z - 1,)),
            dma((Z - 1,)),
            dma((Z - 1,)),
            dma((Z - 1,)),
            dma((Z - 1,)),
            dma((Z - 1,)),
            dma((BLOCKS - 1,)),
            dma((BLOCKS - 1,)),
        ],
        compiler_params=pltpu.CompilerParams(
            collective_id=0, has_side_effects=True, vmem_limit_bytes=60 << 20
        ),
        cost_estimate=pl.CostEstimate(
            flops=5_000_000_000, bytes_accessed=3_700_000, transcendentals=0
        ),
    )(
        token_adapter_index.reshape(1, ROWS),
        adapter_stored_row.reshape(1, -1),
        tokens,
        value_base_weight,
        adapter_down_maps.reshape(HELD, WIDTH),
        adapter_up_maps.reshape(HELD, OUT),
    )


def solution(mesh):
    return jax.shard_map(
        local,
        mesh=mesh,
        in_specs=(
            P("adapter", "tensor"),
            P("adapter"),
            P(),
            P("tensor", None),
            P("adapter", None, "tensor"),
            P("adapter", None, "tensor"),
        ),
        out_specs=P("adapter", "tensor"),
        check_vma=False,
    )
```
